256 devices in a mesh: tm: 16 (over z_hi, x, core), height: 4 (over y), heads: 4 (over z_lo).
Axes of the slice: x: 4, y: 4, z: 8 (z_hi: 2, z_lo: 4; z = z_hi * 4 + z_lo), core: 2. Of those that a mesh axis runs over, the one named last changes fastest.
Arguments:
- query_rows: bfloat16 [32, 4, 384, 3072], P('tm', 'height', None, 'heads'), may hold values from -160 to 160
- key_rows: bfloat16 [32, 4, 384, 3072], P('tm', 'height', None, 'heads'), may hold values from -8 to 8
- value_rows: bfloat16 [32, 4, 384, 3072], P('tm', 'height', None, 'heads'), may hold values from -6 to 6
- out_weight: bfloat16 [3072, 3072], P('heads'), may hold values from -0.109375 to 0.109375
- lengths: int32 [8], replicated, may hold values from 1 to 36, as said below
- radii: int32 [8, 4, 2], replicated, may hold values from 0 to 1
- plan: int32 [16], replicated, may hold values from 0 to 15, each once
Outputs:
- block_output: bfloat16 [32, 4, 384, 3072], P('tm', 'height', None, 'heads')
The draws below stay inside these ranges and needn't reach their ends.
Inputs may be any that keep to these rules, and one draw needn't show every extreme that they name: The tiles ceil(lengths / 6) of all clips add up to 32.
All inputs are finite; a program needn't handle non-finite values.
Results may differ from the reference program's by a relative error of at most 0.0056.
Values may be sent and summed in bfloat16 or wider, within the bound.
No kernel may reach another device: no remote copies, remote signals or barrier semaphores. Data moves between devices by JAX's collectives and lax.ppermute only.
A program may use at most 128 MiB of HBM per device.

```python
import math
import jax
import jax.numpy as jnp
from jax import lax

D = 3072
HEADS = 24
HS = 128
TILE_T = 6
TILE_H = 8
TILE_W = 8
TB = 2
TILE = 384
TT = 32
HT = 4
CLIPS = 8
N_TM = 16


def shared_keys(key):
    return jnp.clip(jax.random.normal(key, (TT, HT, TILE_T * TILE_H * TILE_W, D), jnp.float32), -6.0, 6.0)


def draw_key_rows(key, part):
    base_rows = shared_keys(key)
    return base_rows.astype(jnp.bfloat16)


def draw_query_rows(key, part):
    base_rows = shared_keys(key)
    key = jax.random.fold_in(key, 5)
    drawn_rows = jnp.clip(jax.random.normal(key, base_rows.shape, jnp.float32), -6.0, 6.0)
    return drawn_rows.astype(jnp.bfloat16)


def draw_lengths(key, part):
    key = jax.random.fold_in(key, 7)
    first_key, second_key, third_key, fourth_key = jax.random.split(key, 4)
    base_count = TT // CLIPS
    spread = base_count // 2
    pair_count = CLIPS // 2
    tile_count = jnp.full((CLIPS,), base_count, jnp.int32)
    tile_shift = jax.random.randint(first_key, (pair_count,), -spread, spread + 1).astype(jnp.int32)
    chosen_pair = jax.random.randint(third_key, (), 0, pair_count).astype(jnp.int32)
    sign_bit = jax.random.randint(fourth_key, (), 0, 2).astype(jnp.int32)
    forced = (2 * sign_bit - 1) * spread
    pair_index = jnp.arange(pair_count, dtype=jnp.int32)
    tile_shift = jnp.where(pair_index == chosen_pair, forced, tile_shift).astype(jnp.int32)
    tile_count = tile_count.at[0:2 * pair_count:2].add(tile_shift)
    tile_count = tile_count.at[1:2 * pair_count:2].add(-tile_shift)
    partial_value = jax.random.randint(second_key, (CLIPS,), 1, TILE_T + 1).astype(jnp.int32)
    forced_clip = 2 * chosen_pair + 1 - sign_bit
    partial_value = jnp.where(jnp.arange(CLIPS, dtype=jnp.int32) == forced_clip, TILE_T, partial_value).astype(jnp.int32)
    return (TILE_T * (tile_count - 1) + partial_value).astype(jnp.int32)


def touch_ends(drawn, stream_key, smallest, high):
    place = [jax.random.randint(jax.random.fold_in(stream_key, axis), (), 0, length) for axis, length in enumerate(drawn.shape)]
    longest = drawn.shape.index(max(drawn.shape))
    neighbour = place[:longest] + [(place[longest] + 1) % drawn.shape[longest]] + place[longest + 1:]
    return drawn.at[tuple(place)].set(smallest).at[tuple(neighbour)].set(high)


def steps_of(key, dims, shards, smallest, high):
    factor_of, own = 1.0, jax.random.fold_in(key, 6)
    for axis_at, blocks in shards:
        heights = jnp.exp(jax.random.uniform(jax.random.fold_in(own, axis_at), (blocks,), jnp.float32, smallest / len(shards), high / len(shards)))
        factor_of = factor_of * jnp.repeat(heights, dims[axis_at] // blocks).reshape([-1 if axis == axis_at else 1 for axis in range(len(dims))])
    return factor_of


def scatter_about(stream_key, extent, scale, most, shards=(), kind=jnp.bfloat16):
    gain = steps_of(stream_key, extent, shards, -0.22, 0.18) if shards else 1.0
    values = jax.random.normal(stream_key, extent, jnp.float32) * scale * gain
    return jnp.minimum(jnp.maximum(values, -most), most).astype(kind)


def setup_inputs(seed: int = 0) -> dict:
    key_of = jax.random.split(jax.random.key(seed), 8)
    query_rows = draw_query_rows(jax.random.fold_in(key_of[7], 71), 0)
    key_rows = draw_key_rows(jax.random.fold_in(key_of[7], 71), 0)
    value_rows = scatter_about(key_of[2], (TT, HT, TILE, D), 1.0, 6.0, ((0, 16), (1, 4), (3, 4)))
    out_weight = scatter_about(key_of[3], (D, D), D ** -0.5, 0.109375, ((0, 4),))
    lengths = draw_lengths(jax.random.fold_in(key_of[7], 71), 0)
    radii = touch_ends(jax.random.randint(key_of[5], (CLIPS, HT, 2), 0, 2), jax.random.fold_in(key_of[5], 1), 0, 1).astype(jnp.int32)
    plan = jax.random.permutation(key_of[6], N_TM).astype(jnp.int32)
    return dict(query_rows=query_rows, key_rows=key_rows, value_rows=value_rows, out_weight=out_weight, lengths=lengths, radii=radii, plan=plan)


def tile_tables(lengths, radii, tile_total):
    tile_count = (lengths + TILE_T - 1) // TILE_T
    tile_ends = jnp.cumsum(tile_count).astype(jnp.int32)
    positions = jnp.arange(tile_total, dtype=jnp.int32)
    clip_of = lax.optimization_barrier(jnp.sum((tile_ends[None, :] <= positions[:, None]).astype(jnp.int32), axis=1))
    onehot = (clip_of[:, None] == jnp.arange(lengths.shape[0], dtype=jnp.int32)[None, :]).astype(jnp.int32)
    starts = lax.optimization_barrier(jnp.sum(onehot * (tile_ends - tile_count)[None, :], axis=1))
    frames = lax.optimization_barrier(jnp.sum(onehot * lengths[None, :], axis=1)) - TILE_T * (positions - starts)
    reach_time = lax.optimization_barrier(jnp.sum(onehot[:, :, None] * radii[None, :, :, 0], axis=1))
    reach_height = lax.optimization_barrier(jnp.sum(onehot[:, :, None] * radii[None, :, :, 1], axis=1))
    return (clip_of, frames, reach_time, reach_height)

def reference(query_rows, key_rows, value_rows, out_weight, lengths, radii, plan):
    blocks = jnp.arange(N_TM, dtype=jnp.int32)
    within = jnp.arange(TB, dtype=jnp.int32)
    stored_of_grid = (plan[:, None] * TB + within[None, :]).reshape(-1).astype(jnp.int32)
    holder = lax.optimization_barrier(jnp.sum(jnp.where(plan[:, None] == blocks[None, :], blocks[:, None], 0), axis=0))
    grid_of_stored = (holder[:, None] * TB + within[None, :]).reshape(-1).astype(jnp.int32)
    query_grid = jnp.take(query_rows, stored_of_grid, axis=0)
    key_grid = jnp.take(key_rows, stored_of_grid, axis=0)
    value_grid = jnp.take(value_rows, stored_of_grid, axis=0)
    clip_of, frames, reach_time, reach_height = tile_tables(lengths, radii, TT)
    clip_padded = jnp.pad(clip_of, 1, constant_values=-1)
    frames_padded = jnp.pad(frames, 1)
    key_padded = jnp.pad(key_grid, ((1, 1), (1, 1), (0, 0), (0, 0)))
    value_padded = jnp.pad(value_grid, ((1, 1), (1, 1), (0, 0), (0, 0)))
    frame_of = jnp.arange(TILE, dtype=jnp.int32) // (TILE_H * TILE_W)
    offsets = jnp.arange(3, dtype=jnp.int32) - 1
    zero_index = jnp.zeros((), jnp.int32)
    scale = 1.0 / math.sqrt(HS)

    def one_tile(tile_index):
        time_tile = tile_index // HT
        row_tile = tile_index % HT
        query_tile = lax.dynamic_slice(query_grid, (time_tile, row_tile, zero_index, zero_index), (1, 1, TILE, D))[0, 0]
        key_tile = lax.dynamic_slice(key_padded, (time_tile, row_tile, zero_index, zero_index), (3, 3, TILE, D)).reshape(9 * TILE, D)
        value_tile = lax.dynamic_slice(value_padded, (time_tile, row_tile, zero_index, zero_index), (3, 3, TILE, D)).reshape(9 * TILE, D)
        clip_near = lax.dynamic_slice(clip_padded, (time_tile,), (3,))
        frames_near = lax.dynamic_slice(frames_padded, (time_tile,), (3,))
        own_clip = clip_of[time_tile]
        own_time = reach_time[time_tile, row_tile]
        own_height = reach_height[time_tile, row_tile]
        height_valid = (row_tile + offsets >= 0) & (row_tile + offsets < HT)
        tile_allowed = ((clip_near == own_clip) & (jnp.abs(offsets) <= own_time))[:, None] & ((jnp.abs(offsets) <= own_height) & height_valid)[None, :]
        key_valid = frame_of[None, :] < frames_near[:, None]
        allowed = (tile_allowed[:, :, None] & key_valid[:, None, :]).reshape(9 * TILE)
        query_heads = query_tile.astype(jnp.float32).reshape(TILE, HEADS, HS)
        key_heads = key_tile.astype(jnp.float32).reshape(9 * TILE, HEADS, HS)
        value_heads = value_tile.astype(jnp.float32).reshape(9 * TILE, HEADS, HS)
        scores = jnp.einsum('qhd,khd->hqk', query_heads, key_heads) * scale
        masked = jnp.where(allowed[None, None, :], scores, -jnp.inf)
        largest = lax.optimization_barrier(jnp.max(masked, axis=-1, keepdims=True))
        weights = jnp.exp(masked - largest)
        denominator = lax.optimization_barrier(jnp.sum(weights, axis=-1))
        rounded = lax.optimization_barrier(weights.astype(jnp.bfloat16)).astype(jnp.float32)
        attended = jnp.einsum('hqk,khd->qhd', rounded, value_heads) / denominator.T[:, :, None]
        live_rows = frame_of < frames[time_tile]
        return jnp.where(live_rows[:, None], attended.reshape(TILE, D), 0.0).astype(jnp.bfloat16)
    attended_all = lax.map(one_tile, jnp.arange(TT * HT, dtype=jnp.int32))
    projected = jnp.dot(attended_all.reshape(TT * HT * TILE, D), out_weight, preferred_element_type=jnp.float32)
    block_grid = projected.astype(jnp.bfloat16).reshape(TT, HT, TILE, D)
    return jnp.take(block_grid, grid_of_stored, axis=0)
```

```python
import functools
import math

import jax
import jax.numpy as jnp
from jax import lax
from jax.experimental import pallas as pl
from jax.experimental.pallas import tpu as pltpu
from jax.sharding import PartitionSpec as P

HS = 128
TILE_T = 6
CLIPS = 8
TB = 2
FRAME = 64
TILE = 384
HT = 4
N_TM = 16
GROUP = 8
PIECE = TILE // GROUP
KEEP = 4
LOG2E = 1.4426950408889634

T_KEYS = 0
T_ROWS = 18
T_SEND = 20
T_LOCAL = 36
T_POS = 52
T_SLOT = 68
T_MORE = 84
T_SIZE = 96


def plan_kernel(len_ref, rad_ref, plan_ref, ids_ref, out_ref, clip_ref, frame_ref, hold_ref, need_ref, cnt_ref):
    def zero(i, c):
        out_ref[i] = 0
        return c

    lax.fori_loop(0, T_SIZE, zero, 0)
    start = jnp.int32(0)
    for c in range(CLIPS):
        n = lax.div(len_ref[c] + (TILE_T - 1), jnp.int32(TILE_T))

        def put(t, carry, c=c, start=start):
            clip_ref[t] = c
            frame_ref[t] = jnp.minimum(len_ref[c] - TILE_T * (t - start), TILE_T)
            return carry

        lax.fori_loop(start, jnp.minimum(start + n, TB * N_TM), put, 0)
        start = start + n

    def hold(b, c):
        hold_ref[plan_ref[b]] = b
        return c

    lax.fori_loop(0, N_TM, hold, 0)
    me = ids_ref[0]
    row = ids_ref[1]
    block = hold_ref[me]
    total = TB * N_TM
    for j in range(TB):
        t = block * TB + j
        c = clip_ref[t]
        rt = rad_ref[c * (HT * 2) + row * 2]
        rh = rad_ref[c * (HT * 2) + row * 2 + 1]
        out_ref[T_ROWS + j] = frame_ref[t] * FRAME
        for dt in (-1, 0, 1):
            u = t + dt
            uc = jnp.clip(u, 0, total - 1)
            ok_t = (u >= 0) & (u < total) & (clip_ref[uc] == c) & (abs(dt) <= rt)
            keys = frame_ref[uc] * FRAME
            for dh in (-1, 0, 1):
                ok = ok_t & (row + dh >= 0) & (row + dh < HT) & (abs(dh) <= rh)
                out_ref[T_KEYS + j * 9 + (dt + 1) * 3 + dh + 1] = jnp.where(ok, keys, 0)

    def need_of(b, carry):
        c = clip_ref[b * TB + TB - 1]
        same = c == clip_ref[b * TB + TB]
        near = [rad_ref[c * (HT * 2) + h * 2] >= 1 for h in range(HT)]
        wide = [rad_ref[c * (HT * 2) + h * 2 + 1] >= 1 for h in range(HT)]
        for h in range(HT):
            any_ = near[h]
            for o in (h - 1, h + 1):
                if 0 <= o < HT:
                    any_ = any_ | (near[o] & wide[o])
            need_ref[b * HT + h] = jnp.where(same & any_, 1, 0)
        return carry

    lax.fori_loop(0, N_TM - 1, need_of, 0)
    half = lax.div(me, jnp.int32(GROUP))
    for role in range(2):
        for i in range(2 * HT):
            cnt_ref[i] = 0
        out_ref[T_MORE + role] = 0

        def boundary(b, carry, role=role):
            low, high = plan_ref[b], plan_ref[b + 1]
            src, dst = (low, high) if role == 0 else (high, low)
            sh, dh = lax.div(src, jnp.int32(GROUP)), lax.div(dst, jnp.int32(GROUP))
            sp, dp = src - sh * GROUP, dst - dh * GROUP

            @pl.when((sh == dh) & (dh == half))
            def _():
                out_ref[T_LOCAL + role * GROUP + dp] = 1
                out_ref[T_POS + role * GROUP + dp] = sp

            @pl.when(sh != dh)
            def _():
                for h in range(HT):
                    n = need_ref[b * HT + h]
                    at = cnt_ref[sh * HT + h]
                    hit = (n == 1) & (row == h)

                    @pl.when(hit & (sh == half))
                    def _():
                        out_ref[T_SEND + role * GROUP + at] = sp

                    @pl.when(hit & (dh == half))
                    def _():
                        out_ref[T_SLOT + role * GROUP + dp] = at

                    cnt_ref[sh * HT + h] = at + n

            return carry

        lax.fori_loop(0, N_TM - 1, boundary, 0)
        most = cnt_ref[0]
        for i in range(1, 2 * HT):
            most = jnp.maximum(most, cnt_ref[i])
        out_ref[T_MORE + role] = jnp.where(most > KEEP, 1, 0)


def make_table(lengths, radii, plan, ids):
    smem = pl.BlockSpec(memory_space=pltpu.SMEM)
    return pl.pallas_call(
        plan_kernel,
        out_shape=jax.ShapeDtypeStruct((T_SIZE,), jnp.int32),
        in_specs=[smem] * 4,
        out_specs=smem,
        scratch_shapes=[
            pltpu.SMEM((TB * N_TM,), jnp.int32),
            pltpu.SMEM((TB * N_TM,), jnp.int32),
            pltpu.SMEM((N_TM,), jnp.int32),
            pltpu.SMEM((N_TM * HT,), jnp.int32),
            pltpu.SMEM((2 * HT,), jnp.int32),
        ],
        name="plan_table",
    )(lengths, radii.reshape(-1), plan, ids)


def pick(table, pieces, role, first, count):
    shape = pieces.shape[1:]

    def body(tab, src, dst):
        dst[...] = src[...]

    return pl.pallas_call(
        body,
        grid_spec=pltpu.PrefetchScalarGridSpec(
            num_scalar_prefetch=1,
            grid=(count,),
            in_specs=[
                pl.BlockSpec((1,) + shape, lambda i, tab: (tab[T_SEND + role * GROUP + first + i], 0, 0, 0))
            ],
            out_specs=pl.BlockSpec((1,) + shape, lambda i, tab: (i, 0, 0, 0)),
        ),
        out_shape=jax.ShapeDtypeStruct((count,) + shape, pieces.dtype),
        name="pick_crossing",
    )(table, pieces)


def route(table, pieces, near, far, role):
    shape = pieces.shape[1:]
    at = role * GROUP

    def body(tab, local, keep, rest, dst):
        i = pl.program_id(0)
        is_local = tab[T_LOCAL + at + i] == 1
        slot = tab[T_SLOT + at + i]

        @pl.when(is_local)
        def _():
            dst[...] = local[...]

        @pl.when(jnp.logical_not(is_local) & (slot < KEEP))
        def _():
            dst[...] = keep[...]

        @pl.when(jnp.logical_not(is_local) & (slot >= KEEP))
        def _():
            dst[...] = rest[...]

    block = (1,) + shape
    return pl.pallas_call(
        body,
        grid_spec=pltpu.PrefetchScalarGridSpec(
            num_scalar_prefetch=1,
            grid=(GROUP,),
            in_specs=[
                pl.BlockSpec(block, lambda i, tab: (tab[T_POS + at + i], 0, 0, 0)),
                pl.BlockSpec(block, lambda i, tab: (jnp.minimum(tab[T_SLOT + at + i], KEEP - 1), 0, 0, 0)),
                pl.BlockSpec(block, lambda i, tab: (jnp.maximum(tab[T_SLOT + at + i] - KEEP, 0), 0, 0, 0)),
            ],
            out_specs=pl.BlockSpec(block, lambda i, tab: (i, 0, 0, 0)),
        ),
        out_shape=jax.ShapeDtypeStruct((GROUP,) + shape, pieces.dtype),
        name="route_pieces",
    )(table, pieces, near, far)


def attention_kernel(role, tab, q_ref, k0, v0, ku, vu, kd, vd, e0, eu, ed, out_ref, m_ref, acc_ref):
    factor = LOG2E / math.sqrt(HS)
    q = q_ref[0, 0]
    m_ref[...] = jnp.full(m_ref.shape, -1e30, jnp.float32)
    acc_ref[...] = jnp.zeros(acc_ref.shape, jnp.float32)

    def step(get_k, get_v, keys, masked):
        s = lax.dot_general(get_k(), q, (((1,), (1,)), ((), ())), preferred_element_type=jnp.float32)
        if masked:
            at = lax.broadcasted_iota(jnp.int32, s.shape, 0)
            s = jnp.where(at < keys, s, -1e30)
        old = m_ref[...]
        new = jnp.maximum(old, jnp.max(s, axis=0, keepdims=True))
        m_ref[...] = new
        alpha = jnp.exp2((old - new) * factor)
        p = jnp.exp2((s - new) * factor)
        total = jnp.sum(p, axis=0, keepdims=True)
        v = get_v().T
        o = lax.dot_general(v, p.astype(jnp.bfloat16), (((1,), (0,)), ((), ())), preferred_element_type=jnp.float32)
        acc_ref[0:HS, :] = acc_ref[0:HS, :] * alpha + o
        acc_ref[HS : HS + 1, :] = acc_ref[HS : HS + 1, :] * alpha + total

    own = ((k0, v0), (ku, vu), (kd, vd))
    edges = (e0, eu, ed)
    rows = (0, -1, 1)
    for dt in (0, -1, 1):
        tile = role + dt
        for which, dh in enumerate(rows):
            keys = tab[T_KEYS + role * 9 + (dt + 1) * 3 + dh + 1]
            if 0 <= tile < TB:
                get_k = lambda r=own[which][0], t=tile: r[t, 0]
                get_v = lambda r=own[which][1], t=tile: r[t, 0]
            else:
                get_k = lambda r=edges[which]: r[:, 0].reshape(TILE, HS)
                get_v = lambda r=edges[which]: r[:, 1].reshape(TILE, HS)

            @pl.when(keys == TILE)
            def _(get_k=get_k, get_v=get_v, keys=keys):
                step(get_k, get_v, keys, False)

            @pl.when((keys > 0) & (keys < TILE))
            def _(get_k=get_k, get_v=get_v, keys=keys):
                step(get_k, get_v, keys, True)

    live = lax.broadcasted_iota(jnp.int32, (1, TILE), 1) < tab[T_ROWS + role]
    o = acc_ref[0:HS, :] / acc_ref[HS : HS + 1, :]
    o = jnp.where(live, o, 0.0)
    out_ref[...] = o.T.astype(jnp.bfloat16)


def attention(table, role, q, k0, v0, ku, vu, kd, vd, e0, eu, ed):
    heads = q.shape[3] // HS
    own = pl.BlockSpec((TB, 1, TILE, HS), lambda n, tab: (0, 0, 0, n))
    edge = pl.BlockSpec((GROUP, 2, PIECE, HS), lambda n, tab: (0, 0, 0, n))
    return pl.pallas_call(
        functools.partial(attention_kernel, role),
        grid_spec=pltpu.PrefetchScalarGridSpec(
            num_scalar_prefetch=1,
            grid=(heads,),
            in_specs=[pl.BlockSpec((1, 1, TILE, HS), lambda n, tab: (role, 0, 0, n))] + [own] * 6 + [edge] * 3,
            out_specs=pl.BlockSpec((TILE, HS), lambda n, tab: (0, n)),
            scratch_shapes=[
                pltpu.VMEM((1, TILE), jnp.float32),
                pltpu.VMEM((HS + 8, TILE), jnp.float32),
            ],
        ),
        out_shape=jax.ShapeDtypeStruct((TILE, q.shape[3]), jnp.bfloat16),
        compiler_params=pltpu.CompilerParams(vmem_limit_bytes=32 * 1024 * 1024),
        cost_estimate=pl.CostEstimate(flops=4_000_000_000, bytes_accessed=16_000_000, transcendentals=4_000_000),
        name="tile_attention",
    )(table, q, k0, v0, ku, vu, kd, vd, e0, eu, ed)


def project(attended, weight):
    n = lax.axis_size("heads")
    me = lax.axis_index("heads")
    width = weight.shape[1] // n

    def part(col):
        w = lax.dynamic_slice_in_dim(weight, jnp.clip(col, 0, n - 1) * width, width, 1)
        return jnp.dot(attended, w, preferred_element_type=jnp.float32)

    right, left = None, None
    for s in range(1, n):
        up, down = part(n - s + me), part(me - (n - s))
        if right is not None:
            up, down = up + right.astype(jnp.float32), down + left.astype(jnp.float32)
        right = lax.ppermute(up.astype(jnp.bfloat16), "heads", [(i, i + 1) for i in range(min(s, n - 1))])
        left = lax.ppermute(
            down.astype(jnp.bfloat16), "heads", [(i, i - 1) for i in range(n - 1, max(n - 1 - s, 0), -1)]
        )
    total = part(me) + right.astype(jnp.float32) + left.astype(jnp.float32)
    return total.astype(jnp.bfloat16)


def on_device(query_rows, key_rows, value_rows, out_weight, lengths, radii, plan):
    ids = jnp.stack([lax.axis_index("tm"), lax.axis_index("height")]).astype(jnp.int32)
    table = make_table(lengths, radii, plan, ids)
    up = [(i, i + 1) for i in range(HT - 1)]
    down = [(i + 1, i) for i in range(HT - 1)]
    groups = [list(range(GROUP)), list(range(GROUP, N_TM))]
    swap = [(i, (i + GROUP) % N_TM) for i in range(N_TM)]

    def pieces_of(tile):
        k = key_rows[tile, 0].reshape(GROUP, PIECE, -1)
        v = value_rows[tile, 0].reshape(GROUP, PIECE, -1)
        return jnp.stack([k, v], 1)

    spread = [
        lax.all_to_all(pieces_of(TB - 1 - r), "tm", 0, 0, axis_index_groups=groups, tiled=True) for r in range(2)
    ]
    ku, vu = (lax.ppermute(a, "height", up) for a in (key_rows, value_rows))
    kd, vd = (lax.ppermute(a, "height", down) for a in (key_rows, value_rows))
    edges = []
    for r in range(2):
        near = lax.ppermute(pick(table, spread[r], r, 0, KEEP), "tm", swap)

        def crossing(r=r):
            return lax.ppermute(pick(table, spread[r], r, KEEP, GROUP - KEEP), "tm", swap)

        def none(r=r):
            return jnp.zeros((GROUP - KEEP,) + spread[r].shape[1:], spread[r].dtype)

        far = lax.cond(table[T_MORE + r] > 0, crossing, none)
        routed = route(table, spread[r], near, far, r)
        edge = lax.all_to_all(routed, "tm", 0, 0, axis_index_groups=groups, tiled=True)
        edges.append((edge, lax.ppermute(edge, "height", up), lax.ppermute(edge, "height", down)))
    outs = []
    for r in range(2):
        attended = attention(table, r, query_rows, key_rows, value_rows, ku, vu, kd, vd, *edges[r])
        outs.append(project(attended, out_weight))
    return jnp.stack(outs)[:, None]


def solution(mesh):
    placed = (
        P("tm", "height", None, "heads"),
        P("tm", "height", None, "heads"),
        P("tm", "height", None, "heads"),
        P("heads", None),
        P(),
        P(),
        P(),
    )
    return jax.shard_map(
        on_device,
        mesh=mesh,
        in_specs=placed,
        out_specs=P("tm", "height", None, "heads"),
        check_vma=False,
    )
```

```python
import functools
import math

import jax
import jax.numpy as jnp
from jax import lax
from jax.experimental import pallas as pl
from jax.experimental.pallas import tpu as pltpu
from jax.sharding import PartitionSpec as P

HS = 128
TILE_T = 6
CLIPS = 8
TB = 2
FRAME = 64
TILE = 384
HT = 4
N_TM = 16
GROUP = 8
PIECE = TILE // GROUP
KEEP = 6
MIDDLE = 3
SLOTS = 2 * GROUP
LOG2E = 1.4426950408889634
SMALL = pl.CostEstimate(flops=1000, bytes_accessed=1000, transcendentals=0)

T_KEYS = 0
T_ROWS = 18
T_SEND = 20
T_LOCAL = 36
T_POS = 52
T_SLOT = 68
T_MORE = 84
T_SIZE = 96


def plan_kernel(len_ref, rad_ref, plan_ref, ids_ref, out_ref, clip_ref, frame_ref, hold_ref, need_ref, cnt_ref):
    def zero(i, c):
        out_ref[i] = 0
        return c

    lax.fori_loop(0, T_SIZE, zero, 0)
    start = jnp.int32(0)
    for c in range(CLIPS):
        n = lax.div(len_ref[c] + (TILE_T - 1), jnp.int32(TILE_T))

        def put(t, carry, c=c, start=start):
            clip_ref[t] = c
            frame_ref[t] = jnp.minimum(len_ref[c] - TILE_T * (t - start), TILE_T)
            return carry

        lax.fori_loop(start, jnp.minimum(start + n, TB * N_TM), put, 0)
        start = start + n

    def hold(b, c):
        hold_ref[plan_ref[b]] = b
        return c

    lax.fori_loop(0, N_TM, hold, 0)
    me = ids_ref[0]
    row = ids_ref[1]
    block = hold_ref[me]
    total = TB * N_TM
    for j in range(TB):
        t = block * TB + j
        c = clip_ref[t]
        rt = rad_ref[c * (HT * 2) + row * 2]
        rh = rad_ref[c * (HT * 2) + row * 2 + 1]
        out_ref[T_ROWS + j] = frame_ref[t] * FRAME
        for dt in (-1, 0, 1):
            u = t + dt
            uc = jnp.clip(u, 0, total - 1)
            ok_t = (u >= 0) & (u < total) & (clip_ref[uc] == c) & (abs(dt) <= rt)
            keys = frame_ref[uc] * FRAME
            for dh in (-1, 0, 1):
                ok = ok_t & (row + dh >= 0) & (row + dh < HT) & (abs(dh) <= rh)
                out_ref[T_KEYS + j * 9 + (dt + 1) * 3 + dh + 1] = jnp.where(ok, keys, 0)

    def need_of(b, carry):
        c = clip_ref[b * TB + TB - 1]
        same = c == clip_ref[b * TB + TB]
        near = [rad_ref[c * (HT * 2) + h * 2] >= 1 for h in range(HT)]
        wide = [rad_ref[c * (HT * 2) + h * 2 + 1] >= 1 for h in range(HT)]
        for h in range(HT):
            any_ = near[h]
            for o in (h - 1, h + 1):
                if 0 <= o < HT:
                    any_ = any_ | (near[o] & wide[o])
            need_ref[b * HT + h] = jnp.where(same & any_, 1, 0)
        return carry

    lax.fori_loop(0, N_TM - 1, need_of, 0)
    half = lax.div(me, jnp.int32(GROUP))
    for i in range(2 * HT):
        cnt_ref[i] = 0

    def boundary(b, carry):
        low, high = plan_ref[b], plan_ref[b + 1]
        for role in range(2):
            src, dst = (low, high) if role == 0 else (high, low)
            sh, dh = lax.div(src, jnp.int32(GROUP)), lax.div(dst, jnp.int32(GROUP))
            sp, dp = src - sh * GROUP, dst - dh * GROUP

            @pl.when((sh == dh) & (dh == half))
            def _(role=role, sp=sp, dp=dp):
                out_ref[T_LOCAL + role * GROUP + dp] = 1
                out_ref[T_POS + role * GROUP + dp] = sp

            @pl.when(sh != dh)
            def _(role=role, sp=sp, dp=dp, sh=sh, dh=dh):
                for h in range(HT):
                    n = need_ref[b * HT + h]
                    at = cnt_ref[sh * HT + h]
                    hit = (n == 1) & (row == h)

                    @pl.when(hit & (sh == half))
                    def _():
                        out_ref[T_SEND + at] = 2 * sp + role

                    @pl.when(hit & (dh == half))
                    def _():
                        out_ref[T_SLOT + role * GROUP + dp] = at

                    cnt_ref[sh * HT + h] = at + n

        return carry

    lax.fori_loop(0, N_TM - 1, boundary, 0)
    most = cnt_ref[0]
    for i in range(1, 2 * HT):
        most = jnp.maximum(most, cnt_ref[i])
    out_ref[T_MORE] = jnp.where(most > KEEP + MIDDLE, 2, jnp.where(most > KEEP, 1, 0))


def make_table(lengths, radii, plan, ids):
    smem = pl.BlockSpec(memory_space=pltpu.SMEM)
    return pl.pallas_call(
        plan_kernel,
        out_shape=jax.ShapeDtypeStruct((T_SIZE,), jnp.int32),
        in_specs=[smem] * 4,
        out_specs=smem,
        scratch_shapes=[
            pltpu.SMEM((TB * N_TM,), jnp.int32),
            pltpu.SMEM((TB * N_TM,), jnp.int32),
            pltpu.SMEM((N_TM,), jnp.int32),
            pltpu.SMEM((N_TM * HT,), jnp.int32),
            pltpu.SMEM((2 * HT,), jnp.int32),
        ],
        cost_estimate=SMALL,
        name="plan_table",
    )(lengths, radii.reshape(-1), plan, ids)


def copies(body, name, count, shape, table, *operands):
    whole = pl.BlockSpec(memory_space=pl.ANY)
    return pl.pallas_call(
        body,
        grid_spec=pltpu.PrefetchScalarGridSpec(
            num_scalar_prefetch=1,
            grid=(1,),
            in_specs=[whole] * len(operands),
            out_specs=pl.BlockSpec((count,) + shape, lambda i, tab: (0,) * (len(shape) + 1)),
            scratch_shapes=[pltpu.SemaphoreType.DMA((count,))],
        ),
        out_shape=jax.ShapeDtypeStruct((count,) + shape, operands[0].dtype),
        cost_estimate=SMALL,
        name=name,
    )(table, *operands)


def pick(table, pieces, first, count):
    def body(tab, src, dst, sems):
        work = [
            pltpu.make_async_copy(src.at[tab[T_SEND + first + i]], dst.at[i], sems.at[i]) for i in range(count)
        ]
        for c in work:
            c.start()
        for c in work:
            c.wait()

    return copies(body, "pick_crossing", count, pieces.shape[1:], table, pieces)


def route(table, pieces, near, far, role):
    def body(tab, local, keep, rest, dst, sems):
        for i in range(GROUP):
            is_local = tab[T_LOCAL + role * GROUP + i] == 1
            slot = tab[T_SLOT + role * GROUP + i]

            @pl.when(is_local)
            def _(i=i):
                at = 2 * tab[T_POS + role * GROUP + i] + role
                pltpu.make_async_copy(local.at[at], dst.at[i], sems.at[i]).start()

            @pl.when(jnp.logical_not(is_local) & (slot < KEEP))
            def _(i=i, slot=slot):
                pltpu.make_async_copy(keep.at[jnp.minimum(slot, KEEP - 1)], dst.at[i], sems.at[i]).start()

            @pl.when(jnp.logical_not(is_local) & (slot >= KEEP))
            def _(i=i, slot=slot):
                pltpu.make_async_copy(rest.at[jnp.maximum(slot - KEEP, 0)], dst.at[i], sems.at[i]).start()

        for i in range(GROUP):
            pltpu.make_async_copy(local.at[0], dst.at[i], sems.at[i]).wait()

    return copies(body, "route_pieces", GROUP, pieces.shape[1:], table, pieces, near, far)


def absorb(q, k, v, keys, masked, state_ref):
    factor = LOG2E / math.sqrt(HS)
    heads = range(len(q))
    scores = [
        lax.dot_general(k[h], q[h], (((1,), (1,)), ((), ())), preferred_element_type=jnp.float32) for h in heads
    ]
    for h in heads:
        s = scores[h]
        if masked:
            at = lax.broadcasted_iota(jnp.int32, s.shape, 0)
            s = jnp.where(at < keys, s, -1e30)
        old = state_ref[h, TOP : TOP + 1, :]
        new = jnp.maximum(old, jnp.max(s, axis=0, keepdims=True))
        state_ref[h, TOP : TOP + 1, :] = new
        alpha = jnp.exp2((old - new) * factor)
        p = jnp.exp2((s - new) * factor)
        total = jnp.sum(p, axis=0, keepdims=True)
        o = lax.dot_general(
            v[h].T, p.astype(jnp.bfloat16), (((1,), (0,)), ((), ())), preferred_element_type=jnp.float32
        )
        state_ref[h, 0:HS, :] = state_ref[h, 0:HS, :] * alpha + o
        state_ref[h, HS : HS + 1, :] = state_ref[h, HS : HS + 1, :] * alpha + total


def absorb_if(tab, role, dt, dh, q, get_k, get_v, state_ref):
    keys = tab[T_KEYS + role * 9 + (dt + 1) * 3 + dh + 1]

    @pl.when(keys == TILE)
    def _():
        absorb(q, split(get_k()), split(get_v()), keys, False, state_ref)

    @pl.when((keys > 0) & (keys < TILE))
    def _():
        absorb(q, split(get_k()), split(get_v()), keys, True, state_ref)


TOP = HS + 8
STATE = HS + 16
STEP = 3


def split(x):
    return [x[:, h * HS : (h + 1) * HS] for h in range(STEP)]


def local_kernel(role, tab, q_ref, k0, v0, state_ref):
    q = split(q_ref[0, 0])
    state_ref[:, 0:TOP, :] = jnp.zeros((STEP, TOP, TILE), jnp.float32)
    state_ref[:, TOP:STATE, :] = jnp.full((STEP, STATE - TOP, TILE), -1e30, jnp.float32)
    for tile in (role, 1 - role):
        absorb_if(tab, role, tile - role, 0, q, lambda t=tile: k0[t, 0], lambda t=tile: v0[t, 0], state_ref)


def beside_kernel(role, tab, q_ref, old_ref, ku, vu, kd, vd, state_ref):
    q = split(q_ref[0, 0])
    state_ref[...] = old_ref[...]
    for k, v, dh in ((ku, vu, -1), (kd, vd, 1)):
        for tile in range(TB):
            absorb_if(
                tab, role, tile - role, dh, q, lambda k=k, t=tile: k[t, 0], lambda v=v, t=tile: v[t, 0], state_ref
            )


def edge_kernel(role, tab, q_ref, old_ref, e0, eu, ed, out_ref, state_ref):
    q = split(q_ref[0, 0])
    state_ref[...] = old_ref[...]
    for e, dh in ((e0, 0), (eu, -1), (ed, 1)):
        absorb_if(
            tab,
            role,
            2 * role - 1,
            dh,
            q,
            lambda e=e: e[:, 0].reshape(TILE, STEP * HS),
            lambda e=e: e[:, 1].reshape(TILE, STEP * HS),
            state_ref,
        )
    live = lax.broadcasted_iota(jnp.int32, (1, TILE), 1) < tab[T_ROWS + role]
    for h in range(STEP):
        o = state_ref[h, 0:HS, :] / state_ref[h, HS : HS + 1, :]
        o = jnp.where(live, o, 0.0)
        out_ref[:, h * HS : (h + 1) * HS] = o.T.astype(jnp.bfloat16)


def attend(kernel, name, role, table, query, state, tiles):
    wide = STEP * HS
    spec_of = {
        TILE: pl.BlockSpec((TB, 1, TILE, wide), lambda n, tab: (0, 0, 0, n)),
        PIECE: pl.BlockSpec((GROUP, 2, PIECE, wide), lambda n, tab: (0, 0, 0, n)),
    }
    query_spec = pl.BlockSpec((1, 1, TILE, wide), lambda n, tab: (role, 0, 0, n))
    state_spec = pl.BlockSpec((STEP, STATE, TILE), lambda n, tab: (n, 0, 0))
    heads = query.shape[3] // HS
    last = kernel is edge_kernel
    return pl.pallas_call(
        functools.partial(kernel, role),
        grid_spec=pltpu.PrefetchScalarGridSpec(
            num_scalar_prefetch=1,
            grid=(heads // STEP,),
            in_specs=[query_spec] + [state_spec] * len(state) + [spec_of[t.shape[2]] for t in tiles],
            out_specs=pl.BlockSpec((TILE, wide), lambda n, tab: (0, n)) if last else state_spec,
            scratch_shapes=[pltpu.VMEM((STEP, STATE, TILE), jnp.float32)] if last else [],
        ),
        out_shape=jax.ShapeDtypeStruct((TILE, heads * HS), jnp.bfloat16)
        if last
        else jax.ShapeDtypeStruct((heads, STATE, TILE), jnp.float32),
        compiler_params=pltpu.CompilerParams(vmem_limit_bytes=40 * 1024 * 1024),
        cost_estimate=SMALL,
        name=name,
    )(table, query, *state, *tiles)


class Sums:
    def __init__(self, attended, weight):
        self.n, self.me = lax.axis_size("heads"), lax.axis_index("heads")
        self.width = weight.shape[1] // self.n
        self.attended, self.weight = attended, weight
        self.product = jnp.dot(attended, weight, preferred_element_type=jnp.float32)
        self.step = 0
        self.right, self.left = None, None

    def first(self, col):
        w = lax.dynamic_slice_in_dim(self.weight, jnp.clip(col, 0, self.n - 1) * self.width, self.width, 1)
        return jnp.dot(self.attended, w, preferred_element_type=jnp.float32)

    def part(self, col):
        return lax.dynamic_slice_in_dim(self.product, jnp.clip(col, 0, self.n - 1) * self.width, self.width, 1)

    def add(self):
        self.step += 1
        away = self.n - self.step
        if self.right is None:
            up, down = self.first(self.me + away), self.first(self.me - away)
        else:
            up, down = self.part(self.me + away), self.part(self.me - away)
        if self.right is not None:
            up, down = up + self.right.astype(jnp.float32), down + self.left.astype(jnp.float32)
        self.up, self.down = up.astype(jnp.bfloat16), down.astype(jnp.bfloat16)

    def send(self):
        n, s = self.n, self.step
        self.right = lax.ppermute(self.up, "heads", [(i, i + 1) for i in range(min(s, n - 1))])
        self.left = lax.ppermute(self.down, "heads", [(i, i - 1) for i in range(n - 1, max(n - 1 - s, 0), -1)])

    def finish(self):
        total = self.part(self.me) + self.right.astype(jnp.float32) + self.left.astype(jnp.float32)
        return total.astype(jnp.bfloat16)


def on_device(query_rows, key_rows, value_rows, out_weight, lengths, radii, plan):
    ids = jnp.stack([lax.axis_index("tm"), lax.axis_index("height")]).astype(jnp.int32)
    table = make_table(lengths, radii, plan, ids)
    up = [(i, i + 1) for i in range(HT - 1)]
    down = [(i + 1, i) for i in range(HT - 1)]
    groups = [list(range(GROUP)), list(range(GROUP, N_TM))]
    swap = [(i, (i + GROUP) % N_TM) for i in range(N_TM)]

    tie = lax.optimization_barrier

    def edge_tile(a, tile):
        return a[tile, 0].reshape(GROUP, PIECE, -1)

    pieces = jnp.stack([edge_tile(a, t) for t in (1, 0) for a in (key_rows, value_rows)], 1)
    spread = lax.all_to_all(pieces, "tm", 0, 0, axis_index_groups=groups, tiled=True)
    own_k, own_v, table = tie((key_rows, value_rows, table))
    beside = [lax.ppermute(a, "height", way) for way in (up, down) for a in (own_k, own_v)]
    spread = spread.reshape(SLOTS, 2, PIECE, -1)
    near = lax.ppermute(pick(table, spread, 0, KEEP), "tm", swap)

    def beyond(count):
        rest = SLOTS - KEEP
        if count == 0:
            return jnp.zeros((rest,) + spread.shape[1:], spread.dtype)
        got = lax.ppermute(pick(table, spread, KEEP, count), "tm", swap)
        return got if count == rest else jnp.pad(got, ((0, rest - count), (0, 0), (0, 0), (0, 0)))

    far = lax.switch(table[T_MORE], [functools.partial(beyond, c) for c in (0, MIDDLE, SLOTS - KEEP)])

    def deliver(r):
        routed = route(table, spread, near, far, r)
        return lax.all_to_all(routed, "tm", 0, 0, axis_index_groups=groups, tiled=True)

    def widen(edge):
        return edge, lax.ppermute(edge, "height", up), lax.ppermute(edge, "height", down)

    state = [attend(local_kernel, "attend_local", r, table, query_rows, [], [key_rows, value_rows]) for r in range(2)]
    state[0] = attend(beside_kernel, "attend_beside", 0, table, query_rows, [state[0]], beside)
    near, _ = tie((near, state))
    edge0 = deliver(0)
    wide0 = widen(edge0)
    edge1 = deliver(1)
    wide1 = widen(edge1)
    state[1] = attend(beside_kernel, "attend_beside", 1, table, query_rows, [state[1]], beside)
    wide0, state[1] = tie((wide0, state[1]))
    attended0 = attend(edge_kernel, "attend_edge", 0, table, query_rows, [state[0]], wide0)

    sums0 = Sums(attended0, out_weight)
    sums0.add()
    sums0.send()
    sums0.add()
    wide1, _ = tie((wide1, sums0.up))
    sums0.send()
    attended1 = attend(edge_kernel, "attend_edge", 1, table, query_rows, [state[1]], wide1)
    sums1 = Sums(attended1, out_weight)
    sums1.add()
    sums0.add()
    sums0.send()
    sums1.send()
    sums1.right, sums1.left, sums0.right, sums0.left = tie((sums1.right, sums1.left, sums0.right, sums0.left))
    for _ in range(2):
        sums1.add()
        sums1.up, sums1.down = tie((sums1.up, sums1.down))
        sums1.send()
        sums1.right, sums1.left = tie((sums1.right, sums1.left))
    return jnp.stack([sums0.finish(), sums1.finish()])[:, None]


def solution(mesh):
    placed = (
        P("tm", "height", None, "heads"),
        P("tm", "height", None, "heads"),
        P("tm", "height", None, "heads"),
        P("heads", None),
        P(),
        P(),
        P(),
    )
    return jax.shard_map(
        on_device,
        mesh=mesh,
        in_specs=placed,
        out_specs=P("tm", "height", None, "heads"),
        check_vma=False,
    )
```

```python
import functools
import math

import jax
import jax.numpy as jnp
from jax import lax
from jax.experimental import pallas as pl
from jax.experimental.pallas import tpu as pltpu
from jax.sharding import PartitionSpec as P

HS = 128
TILE_T = 6
CLIPS = 8
TB = 2
FRAME = 64
TILE = 384
HT = 4
N_TM = 16
GROUP = 8
PIECE = TILE // GROUP
KEEP = 4
SLOTS = 2 * GROUP
LOG2E = 1.4426950408889634
SMALL = pl.CostEstimate(flops=1000, bytes_accessed=1000, transcendentals=0)

T_KEYS = 0
T_ROWS = 18
T_SEND = 20
T_LOCAL = 36
T_POS = 52
T_SLOT = 68
T_MORE = 84
T_SIZE = 96


def plan_kernel(len_ref, rad_ref, plan_ref, ids_ref, out_ref, clip_ref, frame_ref, hold_ref, need_ref, cnt_ref):
    def zero(i, c):
        out_ref[i] = 0
        return c

    lax.fori_loop(0, T_SIZE, zero, 0)
    start = jnp.int32(0)
    for c in range(CLIPS):
        n = lax.div(len_ref[c] + (TILE_T - 1), jnp.int32(TILE_T))

        def put(t, carry, c=c, start=start):
            clip_ref[t] = c
            frame_ref[t] = jnp.minimum(len_ref[c] - TILE_T * (t - start), TILE_T)
            return carry

        lax.fori_loop(start, jnp.minimum(start + n, TB * N_TM), put, 0)
        start = start + n

    def hold(b, c):
        hold_ref[plan_ref[b]] = b
        return c

    lax.fori_loop(0, N_TM, hold, 0)
    me = ids_ref[0]
    row = ids_ref[1]
    block = hold_ref[me]
    total = TB * N_TM
    for j in range(TB):
        t = block * TB + j
        c = clip_ref[t]
        rt = rad_ref[c * (HT * 2) + row * 2]
        rh = rad_ref[c * (HT * 2) + row * 2 + 1]
        out_ref[T_ROWS + j] = frame_ref[t] * FRAME
        for dt in (-1, 0, 1):
            u = t + dt
            uc = jnp.clip(u, 0, total - 1)
            ok_t = (u >= 0) & (u < total) & (clip_ref[uc] == c) & (abs(dt) <= rt)
            keys = frame_ref[uc] * FRAME
            for dh in (-1, 0, 1):
                ok = ok_t & (row + dh >= 0) & (row + dh < HT) & (abs(dh) <= rh)
                out_ref[T_KEYS + j * 9 + (dt + 1) * 3 + dh + 1] = jnp.where(ok, keys, 0)

    def need_of(b, carry):
        c = clip_ref[b * TB + TB - 1]
        same = c == clip_ref[b * TB + TB]
        near = [rad_ref[c * (HT * 2) + h * 2] >= 1 for h in range(HT)]
        wide = [rad_ref[c * (HT * 2) + h * 2 + 1] >= 1 for h in range(HT)]
        for h in range(HT):
            any_ = near[h]
            for o in (h - 1, h + 1):
                if 0 <= o < HT:
                    any_ = any_ | (near[o] & wide[o])
            need_ref[b * HT + h] = jnp.where(same & any_, 1, 0)
        return carry

    lax.fori_loop(0, N_TM - 1, need_of, 0)
    half = lax.div(me, jnp.int32(GROUP))
    for role in range(2):
        for i in range(2 * HT):
            cnt_ref[i] = 0
        out_ref[T_MORE + role] = 0

        def boundary(b, carry, role=role):
            low, high = plan_ref[b], plan_ref[b + 1]
            src, dst = (low, high) if role == 0 else (high, low)
            sh, dh = lax.div(src, jnp.int32(GROUP)), lax.div(dst, jnp.int32(GROUP))
            sp, dp = src - sh * GROUP, dst - dh * GROUP

            @pl.when((sh == dh) & (dh == half))
            def _():
                out_ref[T_LOCAL + role * GROUP + dp] = 1
                out_ref[T_POS + role * GROUP + dp] = sp

            @pl.when(sh != dh)
            def _():
                for h in range(HT):
                    n = need_ref[b * HT + h]
                    at = cnt_ref[sh * HT + h]
                    hit = (n == 1) & (row == h)

                    @pl.when(hit & (sh == half))
                    def _():
                        out_ref[T_SEND + role * GROUP + at] = sp

                    @pl.when(hit & (dh == half))
                    def _():
                        out_ref[T_SLOT + role * GROUP + dp] = at

                    cnt_ref[sh * HT + h] = at + n

            return carry

        lax.fori_loop(0, N_TM - 1, boundary, 0)
        most = cnt_ref[0]
        for i in range(1, 2 * HT):
            most = jnp.maximum(most, cnt_ref[i])
        out_ref[T_MORE + role] = jnp.where(most > KEEP, 1, 0)


def make_table(lengths, radii, plan, ids):
    smem = pl.BlockSpec(memory_space=pltpu.SMEM)
    return pl.pallas_call(
        plan_kernel,
        out_shape=jax.ShapeDtypeStruct((T_SIZE,), jnp.int32),
        in_specs=[smem] * 4,
        out_specs=smem,
        scratch_shapes=[
            pltpu.SMEM((TB * N_TM,), jnp.int32),
            pltpu.SMEM((TB * N_TM,), jnp.int32),
            pltpu.SMEM((N_TM,), jnp.int32),
            pltpu.SMEM((N_TM * HT,), jnp.int32),
            pltpu.SMEM((2 * HT,), jnp.int32),
        ],
        cost_estimate=SMALL,
        name="plan_table",
    )(lengths, radii.reshape(-1), plan, ids)


def copies(body, name, count, shape, table, *operands):
    whole = pl.BlockSpec(memory_space=pl.ANY)
    return pl.pallas_call(
        body,
        grid_spec=pltpu.PrefetchScalarGridSpec(
            num_scalar_prefetch=1,
            grid=(1,),
            in_specs=[whole] * len(operands),
            out_specs=pl.BlockSpec((count,) + shape, lambda i, tab: (0,) * (len(shape) + 1)),
            scratch_shapes=[pltpu.SemaphoreType.DMA((count,))],
        ),
        out_shape=jax.ShapeDtypeStruct((count,) + shape, operands[0].dtype),
        cost_estimate=SMALL,
        name=name,
    )(table, *operands)


def pick(table, pieces, role, first, count):
    def body(tab, src, dst, sems):
        work = [
            pltpu.make_async_copy(
                src.at[2 * tab[T_SEND + role * GROUP + first + i] + role], dst.at[i], sems.at[i]
            )
            for i in range(count)
        ]
        for c in work:
            c.start()
        for c in work:
            c.wait()

    return copies(body, "pick_crossing", count, pieces.shape[1:], table, pieces)


def route(table, pieces, near, far, role):
    def body(tab, local, keep, rest, dst, sems):
        for i in range(GROUP):
            is_local = tab[T_LOCAL + role * GROUP + i] == 1
            slot = tab[T_SLOT + role * GROUP + i]

            @pl.when(is_local)
            def _(i=i):
                at = 2 * tab[T_POS + role * GROUP + i] + role
                pltpu.make_async_copy(local.at[at], dst.at[i], sems.at[i]).start()

            @pl.when(jnp.logical_not(is_local) & (slot < KEEP))
            def _(i=i, slot=slot):
                pltpu.make_async_copy(keep.at[jnp.minimum(slot, KEEP - 1)], dst.at[i], sems.at[i]).start()

            @pl.when(jnp.logical_not(is_local) & (slot >= KEEP))
            def _(i=i, slot=slot):
                pltpu.make_async_copy(rest.at[jnp.maximum(slot - KEEP, 0)], dst.at[i], sems.at[i]).start()

        for i in range(GROUP):
            pltpu.make_async_copy(local.at[0], dst.at[i], sems.at[i]).wait()

    return copies(body, "route_pieces", GROUP, pieces.shape[1:], table, pieces, near, far)


def absorb(q, k, v, keys, masked, state_ref):
    factor = LOG2E / math.sqrt(HS)
    heads = range(len(q))
    scores = [
        lax.dot_general(k[h], q[h], (((1,), (1,)), ((), ())), preferred_element_type=jnp.float32) for h in heads
    ]
    for h in heads:
        s = scores[h]
        if masked:
            at = lax.broadcasted_iota(jnp.int32, s.shape, 0)
            s = jnp.where(at < keys, s, -1e30)
        old = state_ref[h, TOP : TOP + 1, :]
        new = jnp.maximum(old, jnp.max(s, axis=0, keepdims=True))
        state_ref[h, TOP : TOP + 1, :] = new
        alpha = jnp.exp2((old - new) * factor)
        p = jnp.exp2((s - new) * factor)
        total = jnp.sum(p, axis=0, keepdims=True)
        o = lax.dot_general(
            v[h].T, p.astype(jnp.bfloat16), (((1,), (0,)), ((), ())), preferred_element_type=jnp.float32
        )
        state_ref[h, 0:HS, :] = state_ref[h, 0:HS, :] * alpha + o
        state_ref[h, HS : HS + 1, :] = state_ref[h, HS : HS + 1, :] * alpha + total


def absorb_if(tab, role, dt, dh, q, get_k, get_v, state_ref):
    keys = tab[T_KEYS + role * 9 + (dt + 1) * 3 + dh + 1]

    @pl.when(keys == TILE)
    def _():
        absorb(q, split(get_k()), split(get_v()), keys, False, state_ref)

    @pl.when((keys > 0) & (keys < TILE))
    def _():
        absorb(q, split(get_k()), split(get_v()), keys, True, state_ref)


TOP = HS + 8
STATE = HS + 16
STEP = 3


def split(x):
    return [x[:, h * HS : (h + 1) * HS] for h in range(STEP)]


def local_kernel(role, tab, q_ref, k0, v0, state_ref):
    q = split(q_ref[0, 0])
    state_ref[:, 0:TOP, :] = jnp.zeros((STEP, TOP, TILE), jnp.float32)
    state_ref[:, TOP:STATE, :] = jnp.full((STEP, STATE - TOP, TILE), -1e30, jnp.float32)
    for tile in (role, 1 - role):
        absorb_if(tab, role, tile - role, 0, q, lambda t=tile: k0[t, 0], lambda t=tile: v0[t, 0], state_ref)


def beside_kernel(role, tab, q_ref, old_ref, ku, vu, kd, vd, state_ref):
    q = split(q_ref[0, 0])
    state_ref[...] = old_ref[...]
    for k, v, dh in ((ku, vu, -1), (kd, vd, 1)):
        for tile in range(TB):
            absorb_if(
                tab, role, tile - role, dh, q, lambda k=k, t=tile: k[t, 0], lambda v=v, t=tile: v[t, 0], state_ref
            )


def edge_kernel(role, tab, q_ref, old_ref, e0, eu, ed, out_ref, state_ref):
    q = split(q_ref[0, 0])
    state_ref[...] = old_ref[...]
    for e, dh in ((e0, 0), (eu, -1), (ed, 1)):
        absorb_if(
            tab,
            role,
            2 * role - 1,
            dh,
            q,
            lambda e=e: e[:, 0].reshape(TILE, STEP * HS),
            lambda e=e: e[:, 1].reshape(TILE, STEP * HS),
            state_ref,
        )
    live = lax.broadcasted_iota(jnp.int32, (1, TILE), 1) < tab[T_ROWS + role]
    for h in range(STEP):
        o = state_ref[h, 0:HS, :] / state_ref[h, HS : HS + 1, :]
        o = jnp.where(live, o, 0.0)
        out_ref[:, h * HS : (h + 1) * HS] = o.T.astype(jnp.bfloat16)


def attend(kernel, name, role, table, query, state, tiles):
    wide = STEP * HS
    spec_of = {
        TILE: pl.BlockSpec((TB, 1, TILE, wide), lambda n, tab: (0, 0, 0, n)),
        PIECE: pl.BlockSpec((GROUP, 2, PIECE, wide), lambda n, tab: (0, 0, 0, n)),
    }
    query_spec = pl.BlockSpec((1, 1, TILE, wide), lambda n, tab: (role, 0, 0, n))
    state_spec = pl.BlockSpec((STEP, STATE, TILE), lambda n, tab: (n, 0, 0))
    heads = query.shape[3] // HS
    last = kernel is edge_kernel
    return pl.pallas_call(
        functools.partial(kernel, role),
        grid_spec=pltpu.PrefetchScalarGridSpec(
            num_scalar_prefetch=1,
            grid=(heads // STEP,),
            in_specs=[query_spec] + [state_spec] * len(state) + [spec_of[t.shape[2]] for t in tiles],
            out_specs=pl.BlockSpec((TILE, wide), lambda n, tab: (0, n)) if last else state_spec,
            scratch_shapes=[pltpu.VMEM((STEP, STATE, TILE), jnp.float32)] if last else [],
        ),
        out_shape=jax.ShapeDtypeStruct((TILE, heads * HS), jnp.bfloat16)
        if last
        else jax.ShapeDtypeStruct((heads, STATE, TILE), jnp.float32),
        compiler_params=pltpu.CompilerParams(vmem_limit_bytes=40 * 1024 * 1024),
        cost_estimate=SMALL,
        name=name,
    )(table, query, *state, *tiles)


class Sums:
    def __init__(self, attended, weight):
        self.n, self.me = lax.axis_size("heads"), lax.axis_index("heads")
        self.width = weight.shape[1] // self.n
        self.attended, self.weight = attended, weight
        self.product = jnp.dot(attended, weight, preferred_element_type=jnp.float32)
        self.step = 0
        self.right, self.left = None, None

    def first(self, col):
        w = lax.dynamic_slice_in_dim(self.weight, jnp.clip(col, 0, self.n - 1) * self.width, self.width, 1)
        return jnp.dot(self.attended, w, preferred_element_type=jnp.float32)

    def part(self, col):
        return lax.dynamic_slice_in_dim(self.product, jnp.clip(col, 0, self.n - 1) * self.width, self.width, 1)

    def add(self):
        self.step += 1
        away = self.n - self.step
        if self.right is None:
            up, down = self.first(self.me + away), self.first(self.me - away)
        else:
            up, down = self.part(self.me + away), self.part(self.me - away)
        if self.right is not None:
            up, down = up + self.right.astype(jnp.float32), down + self.left.astype(jnp.float32)
        self.up, self.down = up.astype(jnp.bfloat16), down.astype(jnp.bfloat16)

    def send(self):
        n, s = self.n, self.step
        self.right = lax.ppermute(self.up, "heads", [(i, i + 1) for i in range(min(s, n - 1))])
        self.left = lax.ppermute(self.down, "heads", [(i, i - 1) for i in range(n - 1, max(n - 1 - s, 0), -1)])

    def finish(self):
        total = self.part(self.me) + self.right.astype(jnp.float32) + self.left.astype(jnp.float32)
        return total.astype(jnp.bfloat16)


def on_device(query_rows, key_rows, value_rows, out_weight, lengths, radii, plan):
    ids = jnp.stack([lax.axis_index("tm"), lax.axis_index("height")]).astype(jnp.int32)
    table = make_table(lengths, radii, plan, ids)
    up = [(i, i + 1) for i in range(HT - 1)]
    down = [(i + 1, i) for i in range(HT - 1)]
    groups = [list(range(GROUP)), list(range(GROUP, N_TM))]
    swap = [(i, (i + GROUP) % N_TM) for i in range(N_TM)]

    tie = lax.optimization_barrier

    def edge_tile(a, tile):
        return a[tile, 0].reshape(GROUP, PIECE, -1)

    pieces = jnp.stack([edge_tile(a, t) for t in (1, 0) for a in (key_rows, value_rows)], 1)
    spread = lax.all_to_all(pieces, "tm", 0, 0, axis_index_groups=groups, tiled=True)
    own_k, own_v, table = tie((key_rows, value_rows, table))
    beside = [lax.ppermute(a, "height", way) for way in (up, down) for a in (own_k, own_v)]
    spread = spread.reshape(SLOTS, 2, PIECE, -1)
    near = [lax.ppermute(pick(table, spread, r, 0, KEEP), "tm", swap) for r in range(2)]

    def beyond(r):
        def crossing():
            return lax.ppermute(pick(table, spread, r, KEEP, GROUP - KEEP), "tm", swap)

        def none():
            return jnp.zeros((GROUP - KEEP,) + spread.shape[1:], spread.dtype)

        return lax.cond(table[T_MORE + r] > 0, crossing, none)

    def deliver(r):
        routed = route(table, spread, near[r], beyond(r), r)
        return lax.all_to_all(routed, "tm", 0, 0, axis_index_groups=groups, tiled=True)

    def widen(edge):
        return edge, lax.ppermute(edge, "height", up), lax.ppermute(edge, "height", down)

    state = [attend(local_kernel, "attend_local", r, table, query_rows, [], [key_rows, value_rows]) for r in range(2)]
    near[0], beside, state = tie((near[0], beside, state))
    edge0 = deliver(0)
    state[0] = attend(beside_kernel, "attend_beside", 0, table, query_rows, [state[0]], beside)
    wide0 = widen(edge0)
    edge1 = deliver(1)
    wide1 = widen(edge1)
    state[1] = attend(beside_kernel, "attend_beside", 1, table, query_rows, [state[1]], beside)
    wide0, state = tie((wide0, state))
    attended0 = attend(edge_kernel, "attend_edge", 0, table, query_rows, [state[0]], wide0)

    sums0 = Sums(attended0, out_weight)
    sums0.add()
    sums0.send()
    sums0.add()
    wide1, _ = tie((wide1, sums0.up))
    sums0.send()
    attended1 = attend(edge_kernel, "attend_edge", 1, table, query_rows, [state[1]], wide1)
    sums1 = Sums(attended1, out_weight)
    sums1.add()
    sums0.add()
    sums0.send()
    sums1.send()
    sums1.add()
    sums1.send()
    sums1.right, sums1.left, sums0.right, sums0.left = tie((sums1.right, sums1.left, sums0.right, sums0.left))
    sums1.add()
    sums1.send()
    return jnp.stack([sums0.finish(), sums1.finish()])[:, None]


def solution(mesh):
    placed = (
        P("tm", "height", None, "heads"),
        P("tm", "height", None, "heads"),
        P("tm", "height", None, "heads"),
        P("heads", None),
        P(),
        P(),
        P(),
    )
    return jax.shard_map(
        on_device,
        mesh=mesh,
        in_specs=placed,
        out_specs=P("tm", "height", None, "heads"),
        check_vma=False,
    )
```

```python
import functools
import math

import jax
import jax.numpy as jnp
from jax import lax
from jax.experimental import pallas as pl
from jax.experimental.pallas import tpu as pltpu
from jax.sharding import PartitionSpec as P

HS = 128
TILE_T = 6
CLIPS = 8
TB = 2
FRAME = 64
TILE = 384
HT = 4
N_TM = 16
GROUP = 8
PIECE = TILE // GROUP
KEEP = 4
SLOTS = 2 * GROUP
LOG2E = 1.4426950408889634
SMALL = pl.CostEstimate(flops=1000, bytes_accessed=1000, transcendentals=0)

T_KEYS = 0
T_ROWS = 18
T_SEND = 20
T_LOCAL = 36
T_POS = 52
T_SLOT = 68
T_MORE = 84
T_SIZE = 96


def plan_kernel(len_ref, rad_ref, plan_ref, ids_ref, out_ref, clip_ref, frame_ref, hold_ref, need_ref, cnt_ref):
    def zero(i, c):
        out_ref[i] = 0
        return c

    lax.fori_loop(0, T_SIZE, zero, 0)
    start = jnp.int32(0)
    for c in range(CLIPS):
        n = lax.div(len_ref[c] + (TILE_T - 1), jnp.int32(TILE_T))

        def put(t, carry, c=c, start=start):
            clip_ref[t] = c
            frame_ref[t] = jnp.minimum(len_ref[c] - TILE_T * (t - start), TILE_T)
            return carry

        lax.fori_loop(start, jnp.minimum(start + n, TB * N_TM), put, 0)
        start = start + n

    def hold(b, c):
        hold_ref[plan_ref[b]] = b
        return c

    lax.fori_loop(0, N_TM, hold, 0)
    me = ids_ref[0]
    row = ids_ref[1]
    block = hold_ref[me]
    total = TB * N_TM
    for j in range(TB):
        t = block * TB + j
        c = clip_ref[t]
        rt = rad_ref[c * (HT * 2) + row * 2]
        rh = rad_ref[c * (HT * 2) + row * 2 + 1]
        out_ref[T_ROWS + j] = frame_ref[t] * FRAME
        for dt in (-1, 0, 1):
            u = t + dt
            uc = jnp.clip(u, 0, total - 1)
            ok_t = (u >= 0) & (u < total) & (clip_ref[uc] == c) & (abs(dt) <= rt)
            keys = frame_ref[uc] * FRAME
            for dh in (-1, 0, 1):
                ok = ok_t & (row + dh >= 0) & (row + dh < HT) & (abs(dh) <= rh)
                out_ref[T_KEYS + j * 9 + (dt + 1) * 3 + dh + 1] = jnp.where(ok, keys, 0)

    def need_of(b, carry):
        c = clip_ref[b * TB + TB - 1]
        same = c == clip_ref[b * TB + TB]
        near = [rad_ref[c * (HT * 2) + h * 2] >= 1 for h in range(HT)]
        wide = [rad_ref[c * (HT * 2) + h * 2 + 1] >= 1 for h in range(HT)]
        for h in range(HT):
            any_ = near[h]
            for o in (h - 1, h + 1):
                if 0 <= o < HT:
                    any_ = any_ | (near[o] & wide[o])
            need_ref[b * HT + h] = jnp.where(same & any_, 1, 0)
        return carry

    lax.fori_loop(0, N_TM - 1, need_of, 0)
    half = lax.div(me, jnp.int32(GROUP))
    for role in range(2):
        for i in range(2 * HT):
            cnt_ref[i] = 0
        out_ref[T_MORE + role] = 0

        def boundary(b, carry, role=role):
            low, high = plan_ref[b], plan_ref[b + 1]
            src, dst = (low, high) if role == 0 else (high, low)
            sh, dh = lax.div(src, jnp.int32(GROUP)), lax.div(dst, jnp.int32(GROUP))
            sp, dp = src - sh * GROUP, dst - dh * GROUP

            @pl.when((sh == dh) & (dh == half))
            def _():
                out_ref[T_LOCAL + role * GROUP + dp] = 1
                out_ref[T_POS + role * GROUP + dp] = sp

            @pl.when(sh != dh)
            def _():
                for h in range(HT):
                    n = need_ref[b * HT + h]
                    at = cnt_ref[sh * HT + h]
                    hit = (n == 1) & (row == h)

                    @pl.when(hit & (sh == half))
                    def _():
                        out_ref[T_SEND + role * GROUP + at] = sp

                    @pl.when(hit & (dh == half))
                    def _():
                        out_ref[T_SLOT + role * GROUP + dp] = at

                    cnt_ref[sh * HT + h] = at + n

            return carry

        lax.fori_loop(0, N_TM - 1, boundary, 0)
        most = cnt_ref[0]
        for i in range(1, 2 * HT):
            most = jnp.maximum(most, cnt_ref[i])
        out_ref[T_MORE + role] = jnp.where(most > KEEP, 1, 0)


def make_table(lengths, radii, plan, ids):
    smem = pl.BlockSpec(memory_space=pltpu.SMEM)
    return pl.pallas_call(
        plan_kernel,
        out_shape=jax.ShapeDtypeStruct((T_SIZE,), jnp.int32),
        in_specs=[smem] * 4,
        out_specs=smem,
        scratch_shapes=[
            pltpu.SMEM((TB * N_TM,), jnp.int32),
            pltpu.SMEM((TB * N_TM,), jnp.int32),
            pltpu.SMEM((N_TM,), jnp.int32),
            pltpu.SMEM((N_TM * HT,), jnp.int32),
            pltpu.SMEM((2 * HT,), jnp.int32),
        ],
        cost_estimate=SMALL,
        name="plan_table",
    )(lengths, radii.reshape(-1), plan, ids)


def copies(body, name, count, shape, table, *operands):
    whole = pl.BlockSpec(memory_space=pl.ANY)
    return pl.pallas_call(
        body,
        grid_spec=pltpu.PrefetchScalarGridSpec(
            num_scalar_prefetch=1,
            grid=(1,),
            in_specs=[whole] * len(operands),
            out_specs=pl.BlockSpec((count,) + shape, lambda i, tab: (0,) * (len(shape) + 1)),
            scratch_shapes=[pltpu.SemaphoreType.DMA((count,))],
        ),
        out_shape=jax.ShapeDtypeStruct((count,) + shape, operands[0].dtype),
        cost_estimate=SMALL,
        name=name,
    )(table, *operands)


def pick(table, pieces, role, first, count):
    def body(tab, src, dst, sems):
        work = [
            pltpu.make_async_copy(
                src.at[2 * tab[T_SEND + role * GROUP + first + i] + role], dst.at[i], sems.at[i]
            )
            for i in range(count)
        ]
        for c in work:
            c.start()
        for c in work:
            c.wait()

    return copies(body, "pick_crossing", count, pieces.shape[1:], table, pieces)


def route(table, pieces, near, far, role):
    def body(tab, local, keep, rest, dst, sems):
        for i in range(GROUP):
            is_local = tab[T_LOCAL + role * GROUP + i] == 1
            slot = tab[T_SLOT + role * GROUP + i]

            @pl.when(is_local)
            def _(i=i):
                at = 2 * tab[T_POS + role * GROUP + i] + role
                pltpu.make_async_copy(local.at[at], dst.at[i], sems.at[i]).start()

            @pl.when(jnp.logical_not(is_local) & (slot < KEEP))
            def _(i=i, slot=slot):
                pltpu.make_async_copy(keep.at[jnp.minimum(slot, KEEP - 1)], dst.at[i], sems.at[i]).start()

            @pl.when(jnp.logical_not(is_local) & (slot >= KEEP))
            def _(i=i, slot=slot):
                pltpu.make_async_copy(rest.at[jnp.maximum(slot - KEEP, 0)], dst.at[i], sems.at[i]).start()

        for i in range(GROUP):
            pltpu.make_async_copy(local.at[0], dst.at[i], sems.at[i]).wait()

    return copies(body, "route_pieces", GROUP, pieces.shape[1:], table, pieces, near, far)


def absorb(q, k, v, keys, masked, state_ref):
    factor = LOG2E / math.sqrt(HS)
    heads = range(len(q))
    scores = [
        lax.dot_general(k[h], q[h], (((1,), (1,)), ((), ())), preferred_element_type=jnp.float32) for h in heads
    ]
    for h in heads:
        s = scores[h]
        if masked:
            at = lax.broadcasted_iota(jnp.int32, s.shape, 0)
            s = jnp.where(at < keys, s, -1e30)
        old = state_ref[h, TOP : TOP + 1, :]
        new = jnp.maximum(old, jnp.max(s, axis=0, keepdims=True))
        state_ref[h, TOP : TOP + 1, :] = new
        alpha = jnp.exp2((old - new) * factor)
        p = jnp.exp2((s - new) * factor)
        total = jnp.sum(p, axis=0, keepdims=True)
        o = lax.dot_general(
            v[h].T, p.astype(jnp.bfloat16), (((1,), (0,)), ((), ())), preferred_element_type=jnp.float32
        )
        state_ref[h, 0:HS, :] = state_ref[h, 0:HS, :] * alpha + o
        state_ref[h, HS : HS + 1, :] = state_ref[h, HS : HS + 1, :] * alpha + total


def absorb_if(tab, role, dt, dh, q, get_k, get_v, state_ref):
    keys = tab[T_KEYS + role * 9 + (dt + 1) * 3 + dh + 1]

    @pl.when(keys == TILE)
    def _():
        absorb(q, split(get_k()), split(get_v()), keys, False, state_ref)

    @pl.when((keys > 0) & (keys < TILE))
    def _():
        absorb(q, split(get_k()), split(get_v()), keys, True, state_ref)


TOP = HS + 8
STATE = HS + 16
STEP = 3


def split(x):
    return [x[:, h * HS : (h + 1) * HS] for h in range(STEP)]


def local_kernel(role, tab, q_ref, k0, v0, state_ref):
    q = split(q_ref[0, 0])
    state_ref[:, 0:TOP, :] = jnp.zeros((STEP, TOP, TILE), jnp.float32)
    state_ref[:, TOP:STATE, :] = jnp.full((STEP, STATE - TOP, TILE), -1e30, jnp.float32)
    for tile in (role, 1 - role):
        absorb_if(tab, role, tile - role, 0, q, lambda t=tile: k0[t, 0], lambda t=tile: v0[t, 0], state_ref)


def beside_kernel(role, tab, q_ref, old_ref, ku, vu, kd, vd, state_ref):
    q = split(q_ref[0, 0])
    state_ref[...] = old_ref[...]
    for k, v, dh in ((ku, vu, -1), (kd, vd, 1)):
        for tile in range(TB):
            absorb_if(
                tab, role, tile - role, dh, q, lambda k=k, t=tile: k[t, 0], lambda v=v, t=tile: v[t, 0], state_ref
            )


def edge_kernel(role, tab, q_ref, old_ref, e0, eu, ed, out_ref, state_ref):
    q = split(q_ref[0, 0])
    state_ref[...] = old_ref[...]
    for e, dh in ((e0, 0), (eu, -1), (ed, 1)):
        absorb_if(
            tab,
            role,
            2 * role - 1,
            dh,
            q,
            lambda e=e: e[:, 0].reshape(TILE, STEP * HS),
            lambda e=e: e[:, 1].reshape(TILE, STEP * HS),
            state_ref,
        )
    live = lax.broadcasted_iota(jnp.int32, (1, TILE), 1) < tab[T_ROWS + role]
    for h in range(STEP):
        o = state_ref[h, 0:HS, :] / state_ref[h, HS : HS + 1, :]
        o = jnp.where(live, o, 0.0)
        out_ref[:, h * HS : (h + 1) * HS] = o.T.astype(jnp.bfloat16)


def attend(kernel, name, role, table, query, state, tiles):
    wide = STEP * HS
    spec_of = {
        TILE: pl.BlockSpec((TB, 1, TILE, wide), lambda n, tab: (0, 0, 0, n)),
        PIECE: pl.BlockSpec((GROUP, 2, PIECE, wide), lambda n, tab: (0, 0, 0, n)),
    }
    query_spec = pl.BlockSpec((1, 1, TILE, wide), lambda n, tab: (role, 0, 0, n))
    state_spec = pl.BlockSpec((STEP, STATE, TILE), lambda n, tab: (n, 0, 0))
    heads = query.shape[3] // HS
    last = kernel is edge_kernel
    return pl.pallas_call(
        functools.partial(kernel, role),
        grid_spec=pltpu.PrefetchScalarGridSpec(
            num_scalar_prefetch=1,
            grid=(heads // STEP,),
            in_specs=[query_spec] + [state_spec] * len(state) + [spec_of[t.shape[2]] for t in tiles],
            out_specs=pl.BlockSpec((TILE, wide), lambda n, tab: (0, n)) if last else state_spec,
            scratch_shapes=[pltpu.VMEM((STEP, STATE, TILE), jnp.float32)] if last else [],
        ),
        out_shape=jax.ShapeDtypeStruct((TILE, heads * HS), jnp.bfloat16)
        if last
        else jax.ShapeDtypeStruct((heads, STATE, TILE), jnp.float32),
        compiler_params=pltpu.CompilerParams(vmem_limit_bytes=40 * 1024 * 1024),
        cost_estimate=SMALL,
        name=name,
    )(table, query, *state, *tiles)


class Sums:
    def __init__(self, attended, weight):
        self.n, self.me = lax.axis_size("heads"), lax.axis_index("heads")
        self.width = weight.shape[1] // self.n
        self.attended, self.weight = attended, weight
        self.product = jnp.dot(attended, weight, preferred_element_type=jnp.float32)
        self.step = 0
        self.right, self.left = None, None

    def first(self, col):
        w = lax.dynamic_slice_in_dim(self.weight, jnp.clip(col, 0, self.n - 1) * self.width, self.width, 1)
        return jnp.dot(self.attended, w, preferred_element_type=jnp.float32)

    def part(self, col):
        return lax.dynamic_slice_in_dim(self.product, jnp.clip(col, 0, self.n - 1) * self.width, self.width, 1)

    def add(self):
        self.step += 1
        away = self.n - self.step
        if self.right is None:
            up, down = self.first(self.me + away), self.first(self.me - away)
        else:
            up, down = self.part(self.me + away), self.part(self.me - away)
        if self.right is not None:
            up, down = up + self.right.astype(jnp.float32), down + self.left.astype(jnp.float32)
        self.up, self.down = up.astype(jnp.bfloat16), down.astype(jnp.bfloat16)

    def send(self):
        n, s = self.n, self.step
        self.right = lax.ppermute(self.up, "heads", [(i, i + 1) for i in range(min(s, n - 1))])
        self.left = lax.ppermute(self.down, "heads", [(i, i - 1) for i in range(n - 1, max(n - 1 - s, 0), -1)])

    def finish(self):
        total = self.part(self.me) + self.right.astype(jnp.float32) + self.left.astype(jnp.float32)
        return total.astype(jnp.bfloat16)


def on_device(query_rows, key_rows, value_rows, out_weight, lengths, radii, plan):
    ids = jnp.stack([lax.axis_index("tm"), lax.axis_index("height")]).astype(jnp.int32)
    table = make_table(lengths, radii, plan, ids)
    up = [(i, i + 1) for i in range(HT - 1)]
    down = [(i + 1, i) for i in range(HT - 1)]
    groups = [list(range(GROUP)), list(range(GROUP, N_TM))]
    swap = [(i, (i + GROUP) % N_TM) for i in range(N_TM)]

    tie = lax.optimization_barrier

    def edge_tile(a, tile):
        return a[tile, 0].reshape(GROUP, PIECE, -1)

    pieces = jnp.stack([edge_tile(a, t) for t in (1, 0) for a in (key_rows, value_rows)], 1)
    spread = lax.all_to_all(pieces, "tm", 0, 0, axis_index_groups=groups, tiled=True)
    own_k, own_v, table = tie((key_rows, value_rows, table))
    beside = [lax.ppermute(a, "height", way) for way in (up, down) for a in (own_k, own_v)]
    spread = spread.reshape(SLOTS, 2, PIECE, -1)
    near = [lax.ppermute(pick(table, spread, r, 0, KEEP), "tm", swap) for r in range(2)]

    def beyond(r):
        def crossing():
            return lax.ppermute(pick(table, spread, r, KEEP, GROUP - KEEP), "tm", swap)

        def none():
            return jnp.zeros((GROUP - KEEP,) + spread.shape[1:], spread.dtype)

        return lax.cond(table[T_MORE + r] > 0, crossing, none)

    def deliver(r):
        routed = route(table, spread, near[r], beyond(r), r)
        return lax.all_to_all(routed, "tm", 0, 0, axis_index_groups=groups, tiled=True)

    def widen(edge):
        return edge, lax.ppermute(edge, "height", up), lax.ppermute(edge, "height", down)

    state = [attend(local_kernel, "attend_local", r, table, query_rows, [], [key_rows, value_rows]) for r in range(2)]
    near[0], beside, state = tie((near[0], beside, state))
    edge0 = deliver(0)
    state[0] = attend(beside_kernel, "attend_beside", 0, table, query_rows, [state[0]], beside)
    wide0 = widen(edge0)
    edge1 = deliver(1)
    wide0, state[0] = tie((wide0, state[0]))
    attended0 = attend(edge_kernel, "attend_edge", 0, table, query_rows, [state[0]], wide0)
    edge1, _ = tie((edge1, attended0))
    wide1 = widen(edge1)
    state[1] = attend(beside_kernel, "attend_beside", 1, table, query_rows, [state[1]], beside)
    wide1, state[1] = tie((wide1, state[1]))

    sums0 = Sums(attended0, out_weight)
    sums0.add()
    sums0.send()
    sums0.add()
    wide1, _ = tie((wide1, sums0.up))
    sums0.send()
    attended1 = attend(edge_kernel, "attend_edge", 1, table, query_rows, [state[1]], wide1)
    sums1 = Sums(attended1, out_weight)
    sums1.add()
    sums0.add()
    sums0.send()
    sums1.send()
    sums1.add()
    sums1.send()
    sums1.right, sums1.left, sums0.right, sums0.left = tie((sums1.right, sums1.left, sums0.right, sums0.left))
    sums1.add()
    sums1.send()
    return jnp.stack([sums0.finish(), sums1.finish()])[:, None]


def solution(mesh):
    placed = (
        P("tm", "height", None, "heads"),
        P("tm", "height", None, "heads"),
        P("tm", "height", None, "heads"),
        P("heads", None),
        P(),
        P(),
        P(),
    )
    return jax.shard_map(
        on_device,
        mesh=mesh,
        in_specs=placed,
        out_specs=P("tm", "height", None, "heads"),
        check_vma=False,
    )
```
